32 devices in a mesh: grp: 2 (over y), row: 4 (over x, core), col: 4 (over z).
Axes of the slice: x: 2, y: 2, z: 4, core: 2. Of those that a mesh axis runs over, the one named last changes fastest.
Arguments:
- stored: bfloat16 [256, 8192], P(('grp', 'row'), 'col'), parts along dimension 0, may hold values from -6 to 6
- gram_old: float32 [16384, 8192], P(('grp', 'row'), 'col'), parts along dimension 0, may hold values from -4 to 4
- w_enc: bfloat16 [8192, 8192], P('col', 'row'), may hold values from -0.0625 to 0.0625
- b_enc: float32 [8192], P('row'), may hold values from -3 to 3
- b_dec: float32 [8192], P('col'), may hold values from -3 to 3
Outputs:
- gram_new: float32 [16384, 8192], P(('grp', 'row'), 'col'), parts along dimension 0
The draws below stay inside these ranges and needn't reach their ends.
There are 2 independent parts, one for each index of `grp`. The reference program is written for one: setup_inputs(seed, part) draws one part's arguments, and reference() takes and returns one part's arrays. A program takes and returns all parts, laid end to end along the dimension named above; an argument that names none is the same for every part. Nothing has to cross between parts.
All inputs are finite; a program needn't handle non-finite values.
Results may differ from the reference program's by a relative error of at most 0.0012.
Values may be sent and summed in bfloat16 or wider, within the bound.
No kernel may reach another device: no remote copies, remote signals or barrier semaphores. Data moves between devices by JAX's collectives and lax.ppermute only.
A program may use at most 128 MiB of HBM per device.

```python
import jax
import jax.numpy as jnp
from jax import lax

D = 8192
W = 8192
SLAB = 128


def level_of(rng, extent, shards, smallest, high):
    level = 1.0
    for axis_at, blocks in shards:
        heights = jax.random.uniform(jax.random.fold_in(jax.random.fold_in(rng, 6), axis_at), (blocks,), jnp.float32, smallest / len(shards), high / len(shards))
        level = level * jnp.repeat(jnp.exp(heights), extent[axis_at] // blocks).reshape((-1,) + (1,) * (len(extent) - 1 - axis_at))
    return level


def normal_values(stream_key, dims, deviation, bound, pieces=(), dtype=jnp.bfloat16):
    entries = jax.random.normal(stream_key, dims, jnp.float32) * deviation
    if len(pieces) > 0:
        entries = level_of(stream_key, dims, pieces, -0.22, 0.18) * entries
    return jnp.clip(entries, min=-bound, max=bound).astype(dtype)


def setup_inputs(seed: int = 0, part: int = 0) -> dict:
    key_of = jax.random.split(jax.random.key(seed), 6)
    part_splits = jax.random.split(jax.random.fold_in(key_of[5], part), 6)
    return {
        "stored": normal_values(part_splits[0], (SLAB, D), 1.0, 6.0, ((0, 4), (1, 4))),
        "gram_old": normal_values(part_splits[1], (W, W), 0.3, 4.0, ((0, 4), (1, 4)), jnp.float32),
        "w_enc": normal_values(key_of[2], (D, W), D ** -0.5, 0.0625, ((0, 4), (1, 4))),
        "b_enc": normal_values(key_of[3], (W,), 0.5, 3.0, ((0, 4),), jnp.float32),
        "b_dec": normal_values(key_of[4], (D,), 0.5, 3.0, ((0, 4),), jnp.float32),
    }


def reference(stored, gram_old, w_enc, b_enc, b_dec):
    centered = (stored.astype(jnp.float32) - b_dec.astype(jnp.float32)[None, :]).astype(jnp.bfloat16)
    pre = jnp.dot(centered, w_enc, preferred_element_type=jnp.float32) + b_enc.astype(jnp.float32)[None, :]
    codes = jnp.maximum(pre, 0.0).astype(jnp.bfloat16)
    product = lax.dot_general(codes, codes, (((0,), (0,)), ((), ())), preferred_element_type=jnp.float32)
    return gram_old + product / SLAB
```

```python
import functools

import jax
import jax.numpy as jnp
from jax import lax
from jax.experimental import pallas as pl
from jax.experimental.pallas import tpu as pltpu
from jax.sharding import PartitionSpec as P

BF16 = jnp.bfloat16
F32 = jnp.float32
CHUNKS = 1
VMEM = pl.BlockSpec(memory_space=pltpu.VMEM)
SMEM = pl.BlockSpec(memory_space=pltpu.SMEM)


def spread(value, axis, source):
    kept = jnp.where(lax.axis_index(axis) == source, value, 0).astype(value.dtype)
    return lax.psum(kept, axis)


def plain(stored, gram_old, w_enc, b_enc, b_dec):
    centered = (stored.astype(F32) - b_dec[None, :]).astype(BF16)
    column = lax.all_gather(centered, "row", axis=0, tiled=True)
    n_col = lax.axis_size("col")
    n_row = lax.axis_size("row")
    partial_sum = jnp.dot(column, w_enc, preferred_element_type=F32)
    totals = lax.psum(partial_sum, "col")
    panel = jnp.maximum(totals + b_enc[None, :], 0.0).astype(BF16)
    ratio = n_col // n_row
    width_sub = panel.shape[1] // ratio
    col_index = lax.axis_index("col")
    mine = lax.dynamic_slice_in_dim(panel, col_index % ratio * width_sub, width_sub, 1)
    other = spread(mine, "row", col_index // ratio)
    product = lax.dot_general(
        panel, other, (((0,), (0,)), ((), ())), preferred_element_type=F32
    )
    return gram_old + product / panel.shape[0]


def flip(value, axis, bit):
    return lax.ppermute(value, axis, [(i, i ^ bit) for i in range(4)])


def center_kernel(at, own, one, two, three, b_dec, out):
    rows = own.shape[0]
    bias = b_dec[...]
    for step, ref in enumerate((own, one, two, three)):
        place = pl.ds(pl.multiple_of((at[0] ^ step) * rows, rows), rows)
        out[place, :] = (ref[...].astype(F32) - bias).astype(BF16)


def center(at, blocks, b_dec):
    rows, depth = blocks[0].shape
    return pl.pallas_call(
        center_kernel,
        out_shape=jax.ShapeDtypeStruct((4 * rows, depth), BF16),
        in_specs=[SMEM] + [VMEM] * 5,
        out_specs=VMEM,
        name="center",
    )(at, *blocks, b_dec[None, :])


def encode_kernel(at, x, w, out):
    out[...] = jnp.dot(x[...], w[...], preferred_element_type=F32).astype(out.dtype)


def encode(piece, x, w, width, dtype):
    rows, depth = x.shape
    tile = min(width, 256)
    per = width // tile
    return pl.pallas_call(
        encode_kernel,
        out_shape=jax.ShapeDtypeStruct((rows, width), dtype),
        grid_spec=pltpu.PrefetchScalarGridSpec(
            num_scalar_prefetch=1,
            grid=(per,),
            in_specs=[
                pl.BlockSpec((rows, depth), lambda j, at: (0, 0)),
                pl.BlockSpec((depth, tile), lambda j, at: (0, at[0] * per + j)),
            ],
            out_specs=pl.BlockSpec((rows, tile), lambda j, at: (0, j)),
        ),
        cost_estimate=pl.CostEstimate(
            flops=2 * rows * depth * width, bytes_accessed=2 * depth * width, transcendentals=0
        ),
        name="encode",
    )(piece, x, w)


def gram_kernel(scale, chunks, at, *refs):
    pieces, (old, out, left, right) = refs[: 4 * chunks], refs[4 * chunks :]
    width = pieces[0].shape[1]
    step = pl.program_id(0)
    tile = out.shape[0]

    @pl.when(step == 0)
    def _():
        for k, ref in enumerate(pieces):
            side, which, chunk = k // (2 * chunks), k // chunks % 2, k % chunks
            index = 2 * chunk + (at[0] ^ which)
            place = pl.ds(pl.multiple_of(index * width, width), width)
            (left, right)[side][:, place] = ref[...]

    rows = left[:, pl.ds(pl.multiple_of(step * tile, tile), tile)]
    product = lax.dot_general(
        rows, right[...], (((0,), (0,)), ((), ())), preferred_element_type=F32
    )
    out[...] = old[...] + product * scale


def gram(half, own, other, own_col, other_col, old):
    chunks = len(own)
    slab, width = own[0].shape
    height, length = old.shape
    tile = 256
    return pl.pallas_call(
        functools.partial(gram_kernel, 1.0 / slab, chunks),
        out_shape=jax.ShapeDtypeStruct(old.shape, F32),
        grid=(height // tile,),
        in_specs=[SMEM] + [VMEM] * (4 * chunks) + [pl.BlockSpec((tile, length), lambda i: (i, 0))],
        out_specs=pl.BlockSpec((tile, length), lambda i: (i, 0)),
        scratch_shapes=[pltpu.VMEM((slab, height), BF16), pltpu.VMEM((slab, length), BF16)],
        compiler_params=pltpu.CompilerParams(vmem_limit_bytes=16 << 20),
        cost_estimate=pl.CostEstimate(
            flops=2 * slab * height * length, bytes_accessed=8 * height * length, transcendentals=0
        ),
        name="gram",
    )(half, *own, *other, *own_col, *other_col, old)


def square(stored, gram_old, w_enc, b_enc, b_dec):
    row, col = lax.axis_index("row"), lax.axis_index("col")
    half = (col & 1).astype(jnp.int32)
    width = w_enc.shape[1] // (2 * CHUNKS)
    one = lambda value: value.astype(jnp.int32)[None]

    across = flip(stored, "row", 2)
    beside = flip(stored, "row", 1)
    slant = flip(across, "row", 1)
    x = center(one(row), (stored, beside, across, slant), b_dec)

    parts = range(CHUNKS)
    mine = [2 * a + half for a in parts]
    theirs = [2 * a + 1 - half for a in parts]
    sent = [flip(encode(one(theirs[a]), x, w_enc, width, BF16), "col", 1) for a in parts]
    kept = [encode(one(mine[a]), x, w_enc, width, F32) for a in parts]
    pair = [kept[a] + sent[a].astype(F32) for a in parts]
    far = [flip(pair[a].astype(BF16), "col", 2) for a in parts]
    bias = [lax.dynamic_slice_in_dim(b_enc, mine[a] * width, width)[None, :] for a in parts]
    own = [
        jnp.maximum(pair[a] + far[a].astype(F32) + bias[a], 0.0).astype(BF16) for a in parts
    ]
    own_x = [flip(own[a], "row", 2) for a in parts]
    other = [flip(own[a], "col", 1) for a in parts]
    other_x = [flip(other[a], "row", 2) for a in parts]

    def column(here, there):
        held = jnp.where(row == col, here, there)
        beside = flip(held, "row", 1)
        return jnp.where((row == col) | ((row ^ 2) == col), held, beside)

    own_col = [column(own[a], own_x[a]) for a in parts]
    other_col = [column(other[a], other_x[a]) for a in parts]
    return gram(one(half), own, other, own_col, other_col, gram_old)


def shards(stored, gram_old, w_enc, b_enc, b_dec):
    if lax.axis_size("row") == 4 and lax.axis_size("col") == 4:
        return square(stored, gram_old, w_enc, b_enc, b_dec)
    return plain(stored, gram_old, w_enc, b_enc, b_dec)


def solution(mesh):
    placed = (
        P(("grp", "row"), "col"),
        P(("grp", "row"), "col"),
        P("col", "row"),
        P("row"),
        P("col"),
    )
    return jax.shard_map(
        shards, mesh=mesh, in_specs=placed, out_specs=P(("grp", "row"), "col"), check_vma=False
    )
```

```python
import jax
import jax.numpy as jnp
from jax import lax
from jax.experimental import pallas as pl
from jax.experimental.pallas import tpu as pltpu
from jax.sharding import PartitionSpec as P

BF16 = jnp.bfloat16
F32 = jnp.float32
MIB = 1 << 20
VMEM = pl.BlockSpec(memory_space=pltpu.VMEM)
SMEM = pl.BlockSpec(memory_space=pltpu.SMEM)
ANY = pl.BlockSpec(memory_space=pl.ANY)


def spread(value, axis, source):
    kept = jnp.where(lax.axis_index(axis) == source, value, 0).astype(value.dtype)
    return lax.psum(kept, axis)


def plain(stored, gram_old, w_enc, b_enc, b_dec):
    centered = (stored.astype(F32) - b_dec[None, :]).astype(BF16)
    column = lax.all_gather(centered, "row", axis=0, tiled=True)
    n_col = lax.axis_size("col")
    n_row = lax.axis_size("row")
    partial_sum = jnp.dot(column, w_enc, preferred_element_type=F32)
    totals = lax.psum(partial_sum, "col")
    panel = jnp.maximum(totals + b_enc[None, :], 0.0).astype(BF16)
    ratio = n_col // n_row
    width_sub = panel.shape[1] // ratio
    col_index = lax.axis_index("col")
    mine = lax.dynamic_slice_in_dim(panel, col_index % ratio * width_sub, width_sub, 1)
    other = spread(mine, "row", col_index // ratio)
    product = lax.dot_general(
        panel, other, (((0,), (0,)), ((), ())), preferred_element_type=F32
    )
    return gram_old + product / panel.shape[0]


def flip(value, axis, bit):
    return lax.ppermute(value, axis, [(i, i ^ bit) for i in range(4)])


def in_hbm(value):
    return pltpu.with_memory_space_constraint(value, pltpu.HBM)


def in_vmem(value):
    return pltpu.with_memory_space_constraint(value, pltpu.VMEM)


def params(mib):
    return pltpu.CompilerParams(vmem_limit_bytes=mib * MIB)


def cost(flops, moved):
    return pl.CostEstimate(flops=flops, bytes_accessed=moved, transcendentals=0)


def struct(shape, dtype):
    return jax.ShapeDtypeStruct(shape, dtype)


TILE = 256
DEPTH_TILE = 512


def row_and_col():
    return lax.axis_index("row"), lax.axis_index("col")


def window(start, size):
    return pl.ds(pl.multiple_of(start, size), size)


def center_into(x, core, here, beside, b_dec):
    rows = here.shape[0]
    for bit, ref in ((0, here), (1, beside)):
        place = window((core ^ bit) * rows, rows)
        x[place, :] = (ref[...].astype(F32) - b_dec[...]).astype(BF16)


def start_loads(half, w, held, sems):
    width = held.shape[1]
    copies = []
    for j in range(held.shape[0] // DEPTH_TILE):
        place = pl.ds(j * DEPTH_TILE, DEPTH_TILE)
        source = w.at[place, window(half * width, width)]
        copies.append(pltpu.make_async_copy(source, held.at[place, :], sems.at[j]))
        copies[-1].start()
    return copies


def dot_as_loaded(copies, x, held):
    total = None
    for j, copy in enumerate(copies):
        copy.wait()
        place = pl.ds(j * DEPTH_TILE, DEPTH_TILE)
        product = jnp.dot(x[:, place], held[place, :], preferred_element_type=F32)
        total = product if total is None else total + product
    return total


def first_send_kernel(here, beside, b_dec, w, out, x, held, sems):
    row, col = row_and_col()
    copies = start_loads(1 - (col & 1), w, held, sems)
    center_into(x, row & 1, here, beside, b_dec)
    out[...] = dot_as_loaded(copies, x, held).astype(BF16)


def first_keep_kernel(x, w, out, held, sems):
    _, col = row_and_col()
    out[...] = dot_as_loaded(start_loads(col & 1, w, held, sems), x, held)


def first_send(here, beside, b_dec, w):
    rows, depth, width = 2 * here.shape[0], here.shape[1], w.shape[1] // 2
    return pl.pallas_call(
        first_send_kernel,
        out_shape=(
            struct((rows, width), BF16),
            struct((rows, depth), BF16),
            struct((depth, width), BF16),
        ),
        in_specs=[VMEM, VMEM, VMEM, ANY],
        out_specs=(VMEM, VMEM, VMEM),
        scratch_shapes=[pltpu.SemaphoreType.DMA((depth // DEPTH_TILE,))],
        compiler_params=params(4),
        cost_estimate=cost(2 * rows * depth * width, 2 * depth * width),
        name="first_send",
    )(here, beside, b_dec, in_hbm(w))


def first_keep(x, w):
    rows, depth, width = x.shape[0], x.shape[1], w.shape[1] // 2
    return pl.pallas_call(
        first_keep_kernel,
        out_shape=(struct((rows, width), F32), struct((depth, width), BF16)),
        in_specs=[VMEM, ANY],
        out_specs=(VMEM, VMEM),
        scratch_shapes=[pltpu.SemaphoreType.DMA((depth // DEPTH_TILE,))],
        compiler_params=params(4),
        cost_estimate=cost(2 * rows * depth * width, 2 * depth * width),
        name="first_keep",
    )(x, in_hbm(w))


def dot_tiles(x, held, out):
    for j in range(out.shape[1] // TILE):
        place = pl.ds(j * TILE, TILE)
        product = jnp.dot(x[...], held[:, place], preferred_element_type=F32)
        out[:, place] = product.astype(out.dtype)


def next_send_kernel(here, beside, b_dec, held, out, x):
    center_into(x, row_and_col()[0] & 1, here, beside, b_dec)
    dot_tiles(x, held, out)


def next_send(here, beside, b_dec, held):
    rows, (depth, width) = 2 * here.shape[0], held.shape
    return pl.pallas_call(
        next_send_kernel,
        out_shape=(struct((rows, width), BF16), struct((rows, depth), BF16)),
        in_specs=[VMEM] * 4,
        out_specs=(VMEM, VMEM),
        compiler_params=params(4),
        cost_estimate=cost(2 * rows * depth * width, 2 * rows * depth),
        name="next_send",
    )(here, beside, b_dec, in_vmem(held))


def next_keep(x, held):
    rows, (depth, width) = x.shape[0], held.shape
    return pl.pallas_call(
        dot_tiles,
        out_shape=struct((rows, width), F32),
        in_specs=[VMEM, VMEM],
        out_specs=VMEM,
        compiler_params=params(4),
        cost_estimate=cost(2 * rows * depth * width, 2 * rows * depth),
        name="next_keep",
    )(x, in_vmem(held))


def small(kernel, name, shape, *operands):
    return pl.pallas_call(
        kernel,
        out_shape=struct(shape, BF16),
        in_specs=[VMEM] * len(operands),
        out_specs=VMEM,
        compiler_params=params(2),
        name=name,
    )(*operands)


def pair_kernel(kept, sent, out):
    out[...] = (kept[...] + sent[...].astype(F32)).astype(BF16)


def codes_kernel(kept, sent, far, b_enc, out):
    width = out.shape[1]
    bias = b_enc[:, window((row_and_col()[1] & 1) * width, width)]
    total = kept[...] + sent[...].astype(F32) + far[...].astype(F32) + bias
    out[...] = jnp.maximum(total, 0.0).astype(BF16)


def choose_kernel(here, there, out):
    row, col = row_and_col()

    @pl.when(row == col)
    def _():
        out[...] = here[...]

    @pl.when(row != col)
    def _():
        out[...] = there[...]


def load_kernel(_, source, out, sem):
    copy = pltpu.make_async_copy(source, out, sem)
    copy.start()
    copy.wait()


def load(after, source):
    return pl.pallas_call(
        load_kernel,
        out_shape=struct(source.shape, source.dtype),
        in_specs=[ANY, ANY],
        out_specs=VMEM,
        scratch_shapes=[pltpu.SemaphoreType.DMA(())],
        compiler_params=params(1),
        cost_estimate=cost(0, 4 * source.size),
        name="load",
    )(after, in_hbm(source))


def gram_kernel(*refs):
    pieces, (old, out, left, right, new, sems) = refs[:12], refs[12:]
    rows, width = pieces[0].shape
    row, col = row_and_col()
    held = (row == col) | ((row ^ 2) == col)
    for k in range(4):
        chunk, other = k // 2, k % 2
        half = window(((col & 1) ^ other) * width, width)
        left[window(((row >> 1) ^ chunk) * rows, rows), half] = pieces[k][...]
        place = window(((col >> 1) ^ chunk) * rows, rows)

        @pl.when(held)
        def _():
            right[place, half] = pieces[4 + k][...]

        @pl.when(jnp.logical_not(held))
        def _():
            right[place, half] = pieces[8 + k][...]

    scale = 1.0 / left.shape[0]
    copies = []
    for i in range(out.shape[0] // TILE):
        tile = pl.ds(i * TILE, TILE)
        product = lax.dot_general(
            left[:, tile], right[...], (((0,), (0,)), ((), ())), preferred_element_type=F32
        )
        new[tile, :] = old[tile, :] + product * scale
        copies.append(pltpu.make_async_copy(new.at[tile, :], out.at[tile, :], sems.at[i]))
        copies[-1].start()
    for copy in copies:
        copy.wait()


def gram(own, held, passed, old):
    height, length = old.shape
    slab = 2 * own[0].shape[0]
    return pl.pallas_call(
        gram_kernel,
        out_shape=struct(old.shape, F32),
        in_specs=[VMEM] * 13,
        out_specs=ANY,
        scratch_shapes=[
            pltpu.VMEM((slab, height), BF16),
            pltpu.VMEM((slab, length), BF16),
            pltpu.VMEM(old.shape, F32),
            pltpu.SemaphoreType.DMA((height // TILE,)),
        ],
        compiler_params=params(24),
        cost_estimate=cost(2 * slab * height * length, 8 * height * length),
        name="gram",
    )(*own, *held, *passed, in_vmem(old))


def after(value, other):
    return lax.optimization_barrier((value, other))[0]


def square(stored, gram_old, w_enc, b_enc, b_dec):
    b_dec, b_enc = b_dec[None, :], b_enc[None, :]

    beside = flip(stored, "row", 1)
    across = flip(stored, "row", 2)
    out_a, x_a, w_out = first_send(stored, beside, b_dec, w_enc)
    sent_a = flip(out_a, "col", 1)
    kept_a, w_keep = first_keep(x_a, w_enc)
    across = after(across, kept_a)
    slant = flip(across, "row", 1)
    out_b, x_b = next_send(across, slant, b_dec, w_out)
    shape = out_a.shape

    def pair_sum(kept, sent):
        return small(pair_kernel, "pair_sum", shape, kept, sent)

    pair_a = pair_sum(kept_a, sent_a)
    sent_b = flip(after(out_b, pair_a), "col", 1)
    far_a = flip(pair_a, "col", 2)
    kept_b = next_keep(x_b, w_keep)
    old = load(pair_a, gram_old)
    pair_b = pair_sum(kept_b, sent_b)
    far_b = flip(after(pair_b, old), "col", 2)

    def finish(kept, sent, far):
        own = small(codes_kernel, "codes", shape, kept, sent, far, b_enc)
        other = flip(own, "col", 1)
        own_x = flip(own, "row", 2)
        other_x = flip(other, "row", 2)
        held_own = small(choose_kernel, "choose", shape, own, own_x)
        held_other = small(choose_kernel, "choose", shape, other, other_x)
        return [own, other], [held_own, held_other]

    far_a = after(far_a, old)
    own_a, held_a = finish(kept_a, sent_a, far_a)
    own_b, held_b = finish(kept_b, sent_b, far_b)
    held = held_a + held_b
    passed = [flip(piece, "row", 1) for piece in held]
    return gram(own_a + own_b, held, passed, old)


def shards(stored, gram_old, w_enc, b_enc, b_dec):
    if lax.axis_size("row") == 4 and lax.axis_size("col") == 4:
        return square(stored, gram_old, w_enc, b_enc, b_dec)
    return plain(stored, gram_old, w_enc, b_enc, b_dec)


def solution(mesh):
    placed = (
        P(("grp", "row"), "col"),
        P(("grp", "row"), "col"),
        P("col", "row"),
        P("row"),
        P("col"),
    )
    return jax.shard_map(
        shards, mesh=mesh, in_specs=placed, out_specs=P(("grp", "row"), "col"), check_vma=False
    )
```

```python
import functools

import jax
import jax.numpy as jnp
from jax import lax
from jax.experimental import pallas as pl
from jax.experimental.pallas import tpu as pltpu
from jax.sharding import PartitionSpec as P

BF16 = jnp.bfloat16
F32 = jnp.float32
MIB = 1 << 20
VMEM = pl.BlockSpec(memory_space=pltpu.VMEM)
SMEM = pl.BlockSpec(memory_space=pltpu.SMEM)
ANY = pl.BlockSpec(memory_space=pl.ANY)


def spread(value, axis, source):
    kept = jnp.where(lax.axis_index(axis) == source, value, 0).astype(value.dtype)
    return lax.psum(kept, axis)


def plain(stored, gram_old, w_enc, b_enc, b_dec):
    centered = (stored.astype(F32) - b_dec[None, :]).astype(BF16)
    column = lax.all_gather(centered, "row", axis=0, tiled=True)
    n_col = lax.axis_size("col")
    n_row = lax.axis_size("row")
    partial_sum = jnp.dot(column, w_enc, preferred_element_type=F32)
    totals = lax.psum(partial_sum, "col")
    panel = jnp.maximum(totals + b_enc[None, :], 0.0).astype(BF16)
    ratio = n_col // n_row
    width_sub = panel.shape[1] // ratio
    col_index = lax.axis_index("col")
    mine = lax.dynamic_slice_in_dim(panel, col_index % ratio * width_sub, width_sub, 1)
    other = spread(mine, "row", col_index // ratio)
    product = lax.dot_general(
        panel, other, (((0,), (0,)), ((), ())), preferred_element_type=F32
    )
    return gram_old + product / panel.shape[0]


def flip(value, axis, bit):
    return lax.ppermute(value, axis, [(i, i ^ bit) for i in range(4)])


def in_hbm(value):
    return pltpu.with_memory_space_constraint(value, pltpu.HBM)


def in_vmem(value):
    return pltpu.with_memory_space_constraint(value, pltpu.VMEM)


def params(mib):
    return pltpu.CompilerParams(vmem_limit_bytes=mib * MIB)


def cost(flops, moved):
    return pl.CostEstimate(flops=flops, bytes_accessed=moved, transcendentals=0)


def struct(shape, dtype):
    return jax.ShapeDtypeStruct(shape, dtype)


TILE = 256
DEPTH_TILE = 512
GRAM_TILE = 128


def row_and_col():
    return lax.axis_index("row"), lax.axis_index("col")


def window(start, size):
    return pl.ds(pl.multiple_of(start, size), size)


def center_into(x, core, here, beside, b_dec):
    rows = here.shape[0]
    for bit, ref in ((0, here), (1, beside)):
        place = window((core ^ bit) * rows, rows)
        x[place, :] = (ref[...].astype(F32) - b_dec[...]).astype(BF16)


def start_loads(half, w, held, sems):
    width = held.shape[1]
    copies = []
    for j in range(held.shape[0] // DEPTH_TILE):
        place = pl.ds(j * DEPTH_TILE, DEPTH_TILE)
        source = w.at[place, window(half * width, width)]
        copies.append(pltpu.make_async_copy(source, held.at[place, :], sems.at[j]))
        copies[-1].start()
    return copies


def dot_as_loaded(copies, x, held):
    total = None
    for j, copy in enumerate(copies):
        copy.wait()
        place = pl.ds(j * DEPTH_TILE, DEPTH_TILE)
        product = jnp.dot(x[:, place], held[place, :], preferred_element_type=F32)
        total = product if total is None else total + product
    return total


def first_keep_kernel(x, w, out, held, sems):
    _, col = row_and_col()
    out[...] = dot_as_loaded(start_loads(col & 1, w, held, sems), x, held)


def load_first_kernel(stored, b_dec, w, stored_out, b_dec_out, held, sems, own_sems):
    own = [
        pltpu.make_async_copy(stored, stored_out, own_sems.at[0]),
        pltpu.make_async_copy(b_dec, b_dec_out, own_sems.at[1]),
    ]
    for copy in own:
        copy.start()
    for copy in start_loads(1 - (row_and_col()[1] & 1), w, held, sems) + own:
        copy.wait()


def load_first(stored, b_dec, w):
    depth, width = w.shape[0], w.shape[1] // 2
    return pl.pallas_call(
        load_first_kernel,
        out_shape=(
            struct(stored.shape, BF16),
            struct(b_dec.shape, F32),
            struct((depth, width), BF16),
        ),
        in_specs=[ANY] * 3,
        out_specs=(VMEM,) * 3,
        scratch_shapes=[
            pltpu.SemaphoreType.DMA((depth // DEPTH_TILE,)),
            pltpu.SemaphoreType.DMA((2,)),
        ],
        compiler_params=params(1),
        cost_estimate=cost(0, 2 * depth * width),
        name="load_first",
    )(in_hbm(stored), in_hbm(b_dec), in_hbm(w))


def first_keep(x, w):
    rows, depth, width = x.shape[0], x.shape[1], w.shape[1] // 2
    return pl.pallas_call(
        first_keep_kernel,
        out_shape=(struct((rows, width), F32), struct((depth, width), BF16)),
        in_specs=[VMEM, ANY],
        out_specs=(VMEM, VMEM),
        scratch_shapes=[pltpu.SemaphoreType.DMA((depth // DEPTH_TILE,))],
        compiler_params=params(4),
        cost_estimate=cost(2 * rows * depth * width, 2 * depth * width),
        name="first_keep",
    )(x, in_hbm(w))


def dot_tiles(x, held, out):
    for j in range(out.shape[1] // TILE):
        place = pl.ds(j * TILE, TILE)
        product = jnp.dot(x[...], held[:, place], preferred_element_type=F32)
        out[:, place] = product.astype(out.dtype)


def send_kernel(here, beside, b_dec, held, out, x):
    center_into(x, row_and_col()[0] & 1, here, beside, b_dec)
    dot_tiles(x, held, out)


def send(here, beside, b_dec, held):
    rows, (depth, width) = 2 * here.shape[0], held.shape
    return pl.pallas_call(
        send_kernel,
        out_shape=(struct((rows, width), BF16), struct((rows, depth), BF16)),
        in_specs=[VMEM] * 4,
        out_specs=(VMEM, VMEM),
        compiler_params=params(4),
        cost_estimate=cost(2 * rows * depth * width, 2 * rows * depth),
        name="send",
    )(here, beside, b_dec, in_vmem(held))


def keep(x, held):
    rows, (depth, width) = x.shape[0], held.shape
    return pl.pallas_call(
        dot_tiles,
        out_shape=struct((rows, width), F32),
        in_specs=[VMEM, VMEM],
        out_specs=VMEM,
        compiler_params=params(4),
        cost_estimate=cost(2 * rows * depth * width, 2 * rows * depth),
        name="keep",
    )(x, in_vmem(held))


def small(kernel, name, shape, *operands):
    return pl.pallas_call(
        kernel,
        out_shape=struct(shape, BF16),
        in_specs=[VMEM] * len(operands),
        out_specs=VMEM,
        compiler_params=params(2),
        name=name,
    )(*operands)


def pair_kernel(kept, sent, out):
    out[...] = (kept[...] + sent[...].astype(F32)).astype(BF16)


def codes_kernel(kept, sent, far, b_enc, out):
    width = out.shape[1]
    bias = b_enc[:, window((row_and_col()[1] & 1) * width, width)]
    total = kept[...] + sent[...].astype(F32) + far[...].astype(F32) + bias
    out[...] = jnp.maximum(total, 0.0).astype(BF16)


def choose_kernel(here, there, out):
    row, col = row_and_col()

    @pl.when(row == col)
    def _():
        out[...] = here[...]

    @pl.when(row != col)
    def _():
        out[...] = there[...]


def load_kernel(part, _, source, out, sem):
    rows = out.shape[0]
    copy = pltpu.make_async_copy(source.at[pl.ds(part * rows, rows), :], out, sem)
    copy.start()
    copy.wait()


def load_half(part, ready, source):
    rows, columns = source.shape[0] // 2, source.shape[1]
    return pl.pallas_call(
        functools.partial(load_kernel, part),
        out_shape=struct((rows, columns), source.dtype),
        in_specs=[ANY, ANY],
        out_specs=VMEM,
        scratch_shapes=[pltpu.SemaphoreType.DMA(())],
        compiler_params=params(1),
        cost_estimate=cost(0, 16 * rows * columns),
        name="load_half",
    )(ready, in_hbm(source))


def gram_kernel(other, *refs):
    pieces, olds, (out, left, right, new, sems) = refs[:8], refs[8:10], refs[-5:]
    rows, width = pieces[0].shape
    row, col = row_and_col()
    held = (row == col) | ((row ^ 2) == col)
    for k in range(4):
        chunk = k // 2
        half = window(((col & 1) ^ (k % 2)) * width, width)
        left[window(((row >> 1) ^ chunk) * rows, rows), half] = pieces[k][...]
    for chunk in range(2):
        place = window(((col >> 1) ^ chunk) * rows, rows)

        @pl.when(held)
        def _():
            right[place, :] = pieces[4 + chunk][...]

        @pl.when(jnp.logical_not(held))
        def _():
            right[place, :] = pieces[6 + chunk][...]

    scale = 1.0 / left.shape[0]
    columns = window(((col & 1) ^ other) * width, width)
    copies = []
    tiles = out.shape[0] // GRAM_TILE
    for i in range(tiles):
        tile = pl.ds(i * GRAM_TILE, GRAM_TILE)
        old, place = olds[i * 2 // tiles], pl.ds(i % (tiles // 2) * GRAM_TILE, GRAM_TILE)
        product = lax.dot_general(
            left[:, tile], right[...], (((0,), (0,)), ((), ())), preferred_element_type=F32
        )
        new[tile, :] = old[place, columns] + product * scale
        copies.append(
            pltpu.make_async_copy(new.at[tile, :], out.at[tile, columns], sems.at[i])
        )
        copies[-1].start()
    for copy in copies:
        copy.wait()


def gram(other, own, held, passed, old, begun=None):
    height, length = 2 * old[0].shape[0], old[0].shape[1]
    rows, width = own[0].shape
    operands = (*own, *held, *passed, *map(in_vmem, old))
    more = () if begun is None else (in_hbm(begun),)
    return pl.pallas_call(
        functools.partial(gram_kernel, other),
        out_shape=struct((height, length), F32),
        in_specs=[VMEM] * len(operands) + [ANY] * len(more),
        out_specs=ANY,
        input_output_aliases={len(operands): 0} if more else {},
        scratch_shapes=[
            pltpu.VMEM((2 * rows, height), BF16),
            pltpu.VMEM((2 * rows, width), BF16),
            pltpu.VMEM((height, width), F32),
            pltpu.SemaphoreType.DMA((height // GRAM_TILE,)),
        ],
        compiler_params=params(16),
        cost_estimate=cost(4 * rows * height * width, 8 * height * width),
        name="gram",
    )(*operands, *more)


def after(value, *others):
    return lax.optimization_barrier((value, *others))[0]


def square(stored, gram_old, w_enc, b_enc, b_dec):
    beside = flip(stored, "row", 1)
    across = flip(stored, "row", 2)
    stored, b_dec, w_out = load_first(stored, b_dec[None, :], w_enc)
    b_enc = b_enc[None, :]
    out_a, x_a = send(stored, beside, b_dec, w_out)
    shape = out_a.shape

    def pair_sum(kept, sent):
        return small(pair_kernel, "pair_sum", shape, kept, sent)

    def codes(kept, sent, far):
        return small(codes_kernel, "codes", shape, kept, sent, far, b_enc)

    def choose(here, there):
        return small(choose_kernel, "choose", shape, here, there)

    sent_a = flip(out_a, "col", 1)
    kept_a, w_keep = first_keep(x_a, w_enc)
    across = after(across, kept_a)
    slant = flip(across, "row", 1)
    pair_a = pair_sum(kept_a, after(sent_a, across))
    far_a = flip(pair_a, "col", 2)
    out_b, x_b = send(across, after(slant, pair_a), b_dec, w_out)
    sent_b = flip(out_b, "col", 1)
    kept_b = keep(x_b, w_keep)
    old_top = load_half(0, kept_b, gram_old)
    far_a = after(far_a, old_top)
    pair_b = pair_sum(kept_b, after(sent_b, far_a))
    far_b = flip(pair_b, "col", 2)
    own_a = codes(kept_a, sent_a, after(far_a, pair_b))
    other_a, own_x_a = flip(own_a, "col", 1), flip(own_a, "row", 2)
    old_bottom = load_half(1, own_a, gram_old)
    far_b = after(far_b, old_bottom)
    other_a, own_x_a = after(other_a, far_b), after(own_x_a, far_b)
    own_b = codes(kept_b, sent_b, far_b)
    other_b, own_x_b = flip(own_b, "col", 1), flip(own_b, "row", 2)
    other_x_a, other_x_b = flip(other_a, "row", 2), flip(other_b, "row", 2)
    rows = [own_a, other_a, own_b, other_b]
    old = [old_top, old_bottom]
    held_own = [choose(own_a, own_x_a), choose(own_b, own_x_b)]
    begun = gram(0, rows, held_own, [flip(piece, "row", 1) for piece in held_own], old)
    held_other = [choose(other_a, other_x_a), choose(other_b, after(other_x_b, begun))]
    passed_other = [flip(piece, "row", 1) for piece in held_other]
    return gram(1, rows, held_other, passed_other, old, begun)


def shards(stored, gram_old, w_enc, b_enc, b_dec):
    if lax.axis_size("row") == 4 and lax.axis_size("col") == 4:
        return square(stored, gram_old, w_enc, b_enc, b_dec)
    return plain(stored, gram_old, w_enc, b_enc, b_dec)


def solution(mesh):
    placed = (
        P(("grp", "row"), "col"),
        P(("grp", "row"), "col"),
        P("col", "row"),
        P("row"),
        P("col"),
    )
    return jax.shard_map(
        shards, mesh=mesh, in_specs=placed, out_specs=P(("grp", "row"), "col"), check_vma=False
    )
```

```python
import functools

import jax
import jax.numpy as jnp
from jax import lax
from jax.experimental import pallas as pl
from jax.experimental.pallas import tpu as pltpu
from jax.sharding import PartitionSpec as P

BF16 = jnp.bfloat16
F32 = jnp.float32
MIB = 1 << 20
VMEM = pl.BlockSpec(memory_space=pltpu.VMEM)
SMEM = pl.BlockSpec(memory_space=pltpu.SMEM)
ANY = pl.BlockSpec(memory_space=pl.ANY)


def spread(value, axis, source):
    kept = jnp.where(lax.axis_index(axis) == source, value, 0).astype(value.dtype)
    return lax.psum(kept, axis)


def plain(stored, gram_old, w_enc, b_enc, b_dec):
    centered = (stored.astype(F32) - b_dec[None, :]).astype(BF16)
    column = lax.all_gather(centered, "row", axis=0, tiled=True)
    n_col = lax.axis_size("col")
    n_row = lax.axis_size("row")
    partial_sum = jnp.dot(column, w_enc, preferred_element_type=F32)
    totals = lax.psum(partial_sum, "col")
    panel = jnp.maximum(totals + b_enc[None, :], 0.0).astype(BF16)
    ratio = n_col // n_row
    width_sub = panel.shape[1] // ratio
    col_index = lax.axis_index("col")
    mine = lax.dynamic_slice_in_dim(panel, col_index % ratio * width_sub, width_sub, 1)
    other = spread(mine, "row", col_index // ratio)
    product = lax.dot_general(
        panel, other, (((0,), (0,)), ((), ())), preferred_element_type=F32
    )
    return gram_old + product / panel.shape[0]


def flip(value, axis, bit):
    return lax.ppermute(value, axis, [(i, i ^ bit) for i in range(4)])


def in_hbm(value):
    return pltpu.with_memory_space_constraint(value, pltpu.HBM)


def in_vmem(value):
    return pltpu.with_memory_space_constraint(value, pltpu.VMEM)


def params(mib):
    return pltpu.CompilerParams(vmem_limit_bytes=mib * MIB)


def cost(flops, moved):
    return pl.CostEstimate(flops=flops, bytes_accessed=moved, transcendentals=0)


def struct(shape, dtype):
    return jax.ShapeDtypeStruct(shape, dtype)


TILE = 256
DEPTH_TILE = 512
GRAM_TILE = 128


def row_and_col():
    return lax.axis_index("row"), lax.axis_index("col")


def window(start, size):
    return pl.ds(pl.multiple_of(start, size), size)


def center_into(x, core, here, beside, b_dec):
    rows = here.shape[0]
    for bit, ref in ((0, here), (1, beside)):
        place = window((core ^ bit) * rows, rows)
        x[place, :] = (ref[...].astype(F32) - b_dec[...]).astype(BF16)


def start_loads(half, w, held, sems):
    width = held.shape[1]
    copies = []
    for j in range(held.shape[0] // DEPTH_TILE):
        place = pl.ds(j * DEPTH_TILE, DEPTH_TILE)
        source = w.at[place, window(half * width, width)]
        copies.append(pltpu.make_async_copy(source, held.at[place, :], sems.at[j]))
        copies[-1].start()
    return copies


def dot_as_loaded(copies, x, held):
    total = None
    for j, copy in enumerate(copies):
        copy.wait()
        place = pl.ds(j * DEPTH_TILE, DEPTH_TILE)
        product = jnp.dot(x[:, place], held[place, :], preferred_element_type=F32)
        total = product if total is None else total + product
    return total


def first_keep_kernel(x, w, out, held, sems):
    _, col = row_and_col()
    out[...] = dot_as_loaded(start_loads(col & 1, w, held, sems), x, held)


def load_first_kernel(stored, b_dec, w, stored_out, b_dec_out, held, sems, own_sems):
    own = [
        pltpu.make_async_copy(stored, stored_out, own_sems.at[0]),
        pltpu.make_async_copy(b_dec, b_dec_out, own_sems.at[1]),
    ]
    for copy in own:
        copy.start()
    for copy in start_loads(1 - (row_and_col()[1] & 1), w, held, sems) + own:
        copy.wait()


def load_first(stored, b_dec, w):
    depth, width = w.shape[0], w.shape[1] // 2
    return pl.pallas_call(
        load_first_kernel,
        out_shape=(
            struct(stored.shape, BF16),
            struct(b_dec.shape, F32),
            struct((depth, width), BF16),
        ),
        in_specs=[ANY] * 3,
        out_specs=(VMEM,) * 3,
        scratch_shapes=[
            pltpu.SemaphoreType.DMA((depth // DEPTH_TILE,)),
            pltpu.SemaphoreType.DMA((2,)),
        ],
        compiler_params=params(1),
        cost_estimate=cost(0, 2 * depth * width),
        name="load_first",
    )(in_hbm(stored), in_hbm(b_dec), in_hbm(w))


def first_keep(x, w):
    rows, depth, width = x.shape[0], x.shape[1], w.shape[1] // 2
    return pl.pallas_call(
        first_keep_kernel,
        out_shape=(struct((rows, width), F32), struct((depth, width), BF16)),
        in_specs=[VMEM, ANY],
        out_specs=(VMEM, VMEM),
        scratch_shapes=[pltpu.SemaphoreType.DMA((depth // DEPTH_TILE,))],
        compiler_params=params(4),
        cost_estimate=cost(2 * rows * depth * width, 2 * depth * width),
        name="first_keep",
    )(x, in_hbm(w))


def dot_tiles(x, held, out):
    for j in range(out.shape[1] // TILE):
        place = pl.ds(j * TILE, TILE)
        product = jnp.dot(x[...], held[:, place], preferred_element_type=F32)
        out[:, place] = product.astype(out.dtype)


def send_kernel(here, beside, b_dec, held, out, x):
    center_into(x, row_and_col()[0] & 1, here, beside, b_dec)
    dot_tiles(x, held, out)


def send(here, beside, b_dec, held):
    rows, (depth, width) = 2 * here.shape[0], held.shape
    return pl.pallas_call(
        send_kernel,
        out_shape=(struct((rows, width), BF16), struct((rows, depth), BF16)),
        in_specs=[VMEM] * 4,
        out_specs=(VMEM, VMEM),
        compiler_params=params(4),
        cost_estimate=cost(2 * rows * depth * width, 2 * rows * depth),
        name="send",
    )(here, beside, b_dec, in_vmem(held))


def keep(x, held):
    rows, (depth, width) = x.shape[0], held.shape
    return pl.pallas_call(
        dot_tiles,
        out_shape=struct((rows, width), F32),
        in_specs=[VMEM, VMEM],
        out_specs=VMEM,
        compiler_params=params(4),
        cost_estimate=cost(2 * rows * depth * width, 2 * rows * depth),
        name="keep",
    )(x, in_vmem(held))


def small(kernel, name, shape, *operands):
    return pl.pallas_call(
        kernel,
        out_shape=struct(shape, BF16),
        in_specs=[VMEM] * len(operands),
        out_specs=VMEM,
        compiler_params=params(2),
        name=name,
    )(*operands)


def pair_kernel(kept, sent, out):
    out[...] = (kept[...] + sent[...].astype(F32)).astype(BF16)


def codes_kernel(kept, sent, far, b_enc, out):
    width = out.shape[1]
    bias = b_enc[:, window((row_and_col()[1] & 1) * width, width)]
    total = kept[...] + sent[...].astype(F32) + far[...].astype(F32) + bias
    out[...] = jnp.maximum(total, 0.0).astype(BF16)


def choose_kernel(here, there, out):
    row, col = row_and_col()

    @pl.when(row == col)
    def _():
        out[...] = here[...]

    @pl.when(row != col)
    def _():
        out[...] = there[...]


def pick_kernel(here, there, out):
    row, col = row_and_col()
    home = (row >> 1) == (col >> 1)

    @pl.when(home)
    def _():
        out[...] = here[...]

    @pl.when(jnp.logical_not(home))
    def _():
        out[...] = there[...]


def same_parity():
    row, col = row_and_col()
    return ((row ^ col) & 1) == 0


def next_kernel(picked, passed, out):
    @pl.when(same_parity())
    def _():
        out[...] = passed[...]

    @pl.when(jnp.logical_not(same_parity()))
    def _():
        out[...] = picked[...]


def load_kernel(part, _, source, out, sem):
    rows = out.shape[0]
    copy = pltpu.make_async_copy(source.at[pl.ds(part * rows, rows), :], out, sem)
    copy.start()
    copy.wait()


def load_half(part, ready, source):
    rows, columns = source.shape[0] // 2, source.shape[1]
    return pl.pallas_call(
        functools.partial(load_kernel, part),
        out_shape=struct((rows, columns), source.dtype),
        in_specs=[ANY, ANY],
        out_specs=VMEM,
        scratch_shapes=[pltpu.SemaphoreType.DMA(())],
        compiler_params=params(1),
        cost_estimate=cost(0, 16 * rows * columns),
        name="load_half",
    )(ready, in_hbm(source))


def gram_kernel(other, *refs):
    pieces, columns, olds = refs[:4], refs[4 : 8 - other], refs[8 - other : 10 - other]
    out, left, right, new, sems = refs[-5:]
    rows, width = pieces[0].shape
    row, col = row_and_col()
    here = ((row == col) | ((row ^ 2) == col), same_parity())
    for k in range(4):
        chunk = k // 2
        half = window(((col & 1) ^ (k % 2)) * width, width)
        left[window(((row >> 1) ^ chunk) * rows, rows), half] = pieces[k][...]
    for chunk in range(2):
        place = window(((col >> 1) ^ chunk) * rows, rows)

        if other and chunk == 1:
            right[place, :] = columns[1][...]
            continue

        @pl.when(here[chunk])
        def _():
            right[place, :] = columns[chunk][...]

        @pl.when(jnp.logical_not(here[chunk]))
        def _():
            right[place, :] = columns[2 + chunk][...]

    scale = 1.0 / left.shape[0]
    span = window(((col & 1) ^ other) * width, width)
    copies = []
    tiles = out.shape[0] // GRAM_TILE
    for i in range(tiles):
        tile = pl.ds(i * GRAM_TILE, GRAM_TILE)
        old, place = olds[i * 2 // tiles], pl.ds(i % (tiles // 2) * GRAM_TILE, GRAM_TILE)
        product = lax.dot_general(
            left[:, tile], right[...], (((0,), (0,)), ((), ())), preferred_element_type=F32
        )
        new[tile, :] = old[place, span] + product * scale
        copies.append(
            pltpu.make_async_copy(new.at[tile, :], out.at[tile, span], sems.at[i])
        )
        copies[-1].start()
    for copy in copies:
        copy.wait()


def gram(other, own, columns, old, begun=None):
    height, length = 2 * old[0].shape[0], old[0].shape[1]
    rows, width = own[0].shape
    operands = (*own, *columns, *map(in_vmem, old))
    more = () if begun is None else (in_hbm(begun),)
    return pl.pallas_call(
        functools.partial(gram_kernel, other),
        out_shape=struct((height, length), F32),
        in_specs=[VMEM] * len(operands) + [ANY] * len(more),
        out_specs=ANY,
        input_output_aliases={len(operands): 0} if more else {},
        scratch_shapes=[
            pltpu.VMEM((2 * rows, height), BF16),
            pltpu.VMEM((2 * rows, width), BF16),
            pltpu.VMEM((height, width), F32),
            pltpu.SemaphoreType.DMA((height // GRAM_TILE,)),
        ],
        compiler_params=params(16),
        cost_estimate=cost(4 * rows * height * width, 8 * height * width),
        name="gram",
    )(*operands, *more)


def after(value, *others):
    return lax.optimization_barrier((value, *others))[0]


def square(stored, gram_old, w_enc, b_enc, b_dec):
    beside = flip(stored, "row", 1)
    across = flip(stored, "row", 2)
    stored, b_dec, w_out = load_first(stored, b_dec[None, :], w_enc)
    b_enc = b_enc[None, :]
    out_a, x_a = send(stored, beside, b_dec, w_out)
    shape = out_a.shape

    def pair_sum(kept, sent):
        return small(pair_kernel, "pair_sum", shape, kept, sent)

    def codes(kept, sent, far):
        return small(codes_kernel, "codes", shape, kept, sent, far, b_enc)

    def choose(here, there):
        return small(choose_kernel, "choose", shape, here, there)

    def pick(here, there):
        return small(pick_kernel, "pick", shape, here, there)

    def next_column(picked, passed):
        return small(next_kernel, "next_column", shape, picked, passed)

    sent_a = flip(out_a, "col", 1)
    kept_a, w_keep = first_keep(x_a, w_enc)
    across = after(across, kept_a)
    slant = flip(across, "row", 1)
    pair_a = pair_sum(kept_a, after(sent_a, across))
    far_a = flip(pair_a, "col", 2)
    out_b, x_b = send(across, after(slant, pair_a), b_dec, w_out)
    sent_b = flip(out_b, "col", 1)
    kept_b = keep(x_b, w_keep)
    old_top = load_half(0, kept_b, gram_old)
    far_a = after(far_a, old_top)
    pair_b = pair_sum(kept_b, after(sent_b, far_a))
    far_b = flip(pair_b, "col", 2)
    own_a = codes(kept_a, sent_a, after(far_a, pair_b))
    other_a, own_x_a = flip(own_a, "col", 1), flip(own_a, "row", 2)
    old_bottom = load_half(1, own_a, gram_old)
    own_x_a = after(own_x_a, old_bottom)
    other_x_a = flip(own_x_a, "col", 1)
    far_b = after(far_b, old_bottom, own_x_a)
    other_a = after(other_a, far_b)
    own_b = codes(kept_b, sent_b, after(far_b, other_a))
    other_b, own_x_b = flip(own_b, "col", 1), flip(own_b, "row", 2)
    held_own_a = choose(own_a, own_x_a)
    passed_own_a = flip(held_own_a, "row", 1)
    held_other_a = choose(other_a, after(other_x_a, own_b))
    passed_other_a = flip(held_other_a, "row", 1)
    pick_b = pick(own_b, after(own_x_b, held_other_a))
    passed_b = after(flip(pick_b, "row", 1), other_b, passed_own_a, passed_other_a)
    column_b = flip(next_column(pick_b, passed_b), "col", 1)
    rows = [own_a, other_a, own_b, other_b]
    old = [old_top, old_bottom]
    begun = gram(0, rows, [held_own_a, pick_b, passed_own_a, passed_b], old)
    columns = [held_other_a, after(column_b, begun), passed_other_a]
    return gram(1, rows, columns, old, begun)


def shards(stored, gram_old, w_enc, b_enc, b_dec):
    if lax.axis_size("row") == 4 and lax.axis_size("col") == 4:
        return square(stored, gram_old, w_enc, b_enc, b_dec)
    return plain(stored, gram_old, w_enc, b_enc, b_dec)


def solution(mesh):
    placed = (
        P(("grp", "row"), "col"),
        P(("grp", "row"), "col"),
        P("col", "row"),
        P("row"),
        P("col"),
    )
    return jax.shard_map(
        shards, mesh=mesh, in_specs=placed, out_specs=P(("grp", "row"), "col"), check_vma=False
    )
```

```python
import functools

import jax
import jax.numpy as jnp
from jax import lax
from jax.experimental import pallas as pl
from jax.experimental.pallas import tpu as pltpu
from jax.sharding import PartitionSpec as P

BF16 = jnp.bfloat16
F32 = jnp.float32
MIB = 1 << 20
VMEM = pl.BlockSpec(memory_space=pltpu.VMEM)
SMEM = pl.BlockSpec(memory_space=pltpu.SMEM)
ANY = pl.BlockSpec(memory_space=pl.ANY)


def spread(value, axis, source):
    kept = jnp.where(lax.axis_index(axis) == source, value, 0).astype(value.dtype)
    return lax.psum(kept, axis)


def plain(stored, gram_old, w_enc, b_enc, b_dec):
    centered = (stored.astype(F32) - b_dec[None, :]).astype(BF16)
    column = lax.all_gather(centered, "row", axis=0, tiled=True)
    n_col = lax.axis_size("col")
    n_row = lax.axis_size("row")
    partial_sum = jnp.dot(column, w_enc, preferred_element_type=F32)
    totals = lax.psum(partial_sum, "col")
    panel = jnp.maximum(totals + b_enc[None, :], 0.0).astype(BF16)
    ratio = n_col // n_row
    width_sub = panel.shape[1] // ratio
    col_index = lax.axis_index("col")
    mine = lax.dynamic_slice_in_dim(panel, col_index % ratio * width_sub, width_sub, 1)
    other = spread(mine, "row", col_index // ratio)
    product = lax.dot_general(
        panel, other, (((0,), (0,)), ((), ())), preferred_element_type=F32
    )
    return gram_old + product / panel.shape[0]


def flip(value, axis, bit):
    return lax.ppermute(value, axis, [(i, i ^ bit) for i in range(4)])


def in_hbm(value):
    return pltpu.with_memory_space_constraint(value, pltpu.HBM)


def in_vmem(value):
    return pltpu.with_memory_space_constraint(value, pltpu.VMEM)


def params(mib):
    return pltpu.CompilerParams(vmem_limit_bytes=mib * MIB)


def cost(flops, moved):
    return pl.CostEstimate(flops=flops, bytes_accessed=moved, transcendentals=0)


def struct(shape, dtype):
    return jax.ShapeDtypeStruct(shape, dtype)


TILE = 256
DEPTH_TILE = 512
GRAM_TILE = 128


def row_and_col():
    return lax.axis_index("row"), lax.axis_index("col")


def window(start, size):
    return pl.ds(pl.multiple_of(start, size), size)


def center_into(x, core, here, beside, b_dec):
    rows = here.shape[0]
    for bit, ref in ((0, here), (1, beside)):
        place = window((core ^ bit) * rows, rows)
        x[place, :] = (ref[...].astype(F32) - b_dec[...]).astype(BF16)


def start_loads(half, w, held, sems):
    width = held.shape[1]
    copies = []
    for j in range(held.shape[0] // DEPTH_TILE):
        place = pl.ds(j * DEPTH_TILE, DEPTH_TILE)
        source = w.at[place, window(half * width, width)]
        copies.append(pltpu.make_async_copy(source, held.at[place, :], sems.at[j]))
        copies[-1].start()
    return copies


def dot_as_loaded(copies, x, held):
    total = None
    for j, copy in enumerate(copies):
        copy.wait()
        place = pl.ds(j * DEPTH_TILE, DEPTH_TILE)
        product = jnp.dot(x[:, place], held[place, :], preferred_element_type=F32)
        total = product if total is None else total + product
    return total


def first_keep_kernel(x, w, out, held, sems):
    _, col = row_and_col()
    out[...] = dot_as_loaded(start_loads(col & 1, w, held, sems), x, held)


def load_first_kernel(stored, b_dec, w, stored_out, b_dec_out, held, sems, own_sems):
    own = [
        pltpu.make_async_copy(stored, stored_out, own_sems.at[0]),
        pltpu.make_async_copy(b_dec, b_dec_out, own_sems.at[1]),
    ]
    for copy in own:
        copy.start()
    for copy in start_loads(1 - (row_and_col()[1] & 1), w, held, sems) + own:
        copy.wait()


def load_first(stored, b_dec, w):
    depth, width = w.shape[0], w.shape[1] // 2
    return pl.pallas_call(
        load_first_kernel,
        out_shape=(
            struct(stored.shape, BF16),
            struct(b_dec.shape, F32),
            struct((depth, width), BF16),
        ),
        in_specs=[ANY] * 3,
        out_specs=(VMEM,) * 3,
        scratch_shapes=[
            pltpu.SemaphoreType.DMA((depth // DEPTH_TILE,)),
            pltpu.SemaphoreType.DMA((2,)),
        ],
        compiler_params=params(1),
        cost_estimate=cost(0, 2 * depth * width),
        name="load_first",
    )(in_hbm(stored), in_hbm(b_dec), in_hbm(w))


def first_keep(x, w):
    rows, depth, width = x.shape[0], x.shape[1], w.shape[1] // 2
    return pl.pallas_call(
        first_keep_kernel,
        out_shape=(struct((rows, width), F32), struct((depth, width), BF16)),
        in_specs=[VMEM, ANY],
        out_specs=(VMEM, VMEM),
        scratch_shapes=[pltpu.SemaphoreType.DMA((depth // DEPTH_TILE,))],
        compiler_params=params(4),
        cost_estimate=cost(2 * rows * depth * width, 2 * depth * width),
        name="first_keep",
    )(x, in_hbm(w))


def dot_tiles(x, held, out):
    for j in range(out.shape[1] // TILE):
        place = pl.ds(j * TILE, TILE)
        product = jnp.dot(x[...], held[:, place], preferred_element_type=F32)
        out[:, place] = product.astype(out.dtype)


def send_kernel(here, beside, b_dec, held, out, x):
    center_into(x, row_and_col()[0] & 1, here, beside, b_dec)
    dot_tiles(x, held, out)


def send(here, beside, b_dec, held):
    rows, (depth, width) = 2 * here.shape[0], held.shape
    return pl.pallas_call(
        send_kernel,
        out_shape=(struct((rows, width), BF16), struct((rows, depth), BF16)),
        in_specs=[VMEM] * 4,
        out_specs=(VMEM, VMEM),
        compiler_params=params(4),
        cost_estimate=cost(2 * rows * depth * width, 2 * rows * depth),
        name="send",
    )(here, beside, b_dec, in_vmem(held))


def keep(x, held):
    rows, (depth, width) = x.shape[0], held.shape
    return pl.pallas_call(
        dot_tiles,
        out_shape=struct((rows, width), F32),
        in_specs=[VMEM, VMEM],
        out_specs=VMEM,
        compiler_params=params(4),
        cost_estimate=cost(2 * rows * depth * width, 2 * rows * depth),
        name="keep",
    )(x, in_vmem(held))


def small(kernel, name, shape, *operands):
    return pl.pallas_call(
        kernel,
        out_shape=struct(shape, BF16),
        in_specs=[VMEM] * len(operands),
        out_specs=VMEM,
        compiler_params=params(2),
        name=name,
    )(*operands)


def pair_kernel(kept, sent, out):
    out[...] = (kept[...] + sent[...].astype(F32)).astype(BF16)


def codes_kernel(kept, sent, far, b_enc, out):
    width = out.shape[1]
    bias = b_enc[:, window((row_and_col()[1] & 1) * width, width)]
    total = kept[...] + sent[...].astype(F32) + far[...].astype(F32) + bias
    out[...] = jnp.maximum(total, 0.0).astype(BF16)


def choose_kernel(here, there, out):
    row, col = row_and_col()

    @pl.when(row == col)
    def _():
        out[...] = here[...]

    @pl.when(row != col)
    def _():
        out[...] = there[...]


def pick_kernel(here, there, out):
    row, col = row_and_col()
    home = (row >> 1) == (col >> 1)

    @pl.when(home)
    def _():
        out[...] = here[...]

    @pl.when(jnp.logical_not(home))
    def _():
        out[...] = there[...]


def same_parity():
    row, col = row_and_col()
    return ((row ^ col) & 1) == 0


def next_kernel(picked, passed, out):
    @pl.when(same_parity())
    def _():
        out[...] = passed[...]

    @pl.when(jnp.logical_not(same_parity()))
    def _():
        out[...] = picked[...]


def load_kernel(part, _, source, out, sem):
    rows = out.shape[0]
    copy = pltpu.make_async_copy(source.at[pl.ds(part * rows, rows), :], out, sem)
    copy.start()
    copy.wait()


def load_half(part, ready, source):
    rows, columns = source.shape[0] // 2, source.shape[1]
    return pl.pallas_call(
        functools.partial(load_kernel, part),
        out_shape=struct((rows, columns), source.dtype),
        in_specs=[ANY, ANY],
        out_specs=VMEM,
        scratch_shapes=[pltpu.SemaphoreType.DMA(())],
        compiler_params=params(1),
        cost_estimate=cost(0, 16 * rows * columns),
        name="load_half",
    )(ready, in_hbm(source))


def gram_kernel(other, *refs):
    pieces, columns, olds = refs[:4], refs[4 : 8 - other], refs[8 - other : 10 - other]
    out, left, right, new, sems = refs[-5:]
    rows, width = pieces[0].shape
    row, col = row_and_col()
    here = ((row == col) | ((row ^ 2) == col), same_parity())
    for k in range(4):
        chunk = k // 2
        half = window(((col & 1) ^ (k % 2)) * width, width)
        left[window(((row >> 1) ^ chunk) * rows, rows), half] = pieces[k][...]
    for chunk in range(2):
        place = window(((col >> 1) ^ chunk) * rows, rows)

        if other and chunk == 1:
            right[place, :] = columns[1][...]
            continue

        @pl.when(here[chunk])
        def _():
            right[place, :] = columns[chunk][...]

        @pl.when(jnp.logical_not(here[chunk]))
        def _():
            right[place, :] = columns[2 + chunk][...]

    scale = 1.0 / left.shape[0]
    span = window(((col & 1) ^ other) * width, width)
    copies = []
    tiles = out.shape[0] // GRAM_TILE
    for i in range(tiles):
        tile = pl.ds(i * GRAM_TILE, GRAM_TILE)
        old, place = olds[i * 2 // tiles], pl.ds(i % (tiles // 2) * GRAM_TILE, GRAM_TILE)
        product = lax.dot_general(
            left[:, tile], right[...], (((0,), (0,)), ((), ())), preferred_element_type=F32
        )
        new[tile, :] = old[place, span] + product * scale
        copies.append(
            pltpu.make_async_copy(new.at[tile, :], out.at[tile, span], sems.at[i])
        )
        copies[-1].start()
    for copy in copies:
        copy.wait()


def gram(other, own, columns, old, begun=None):
    height, length = 2 * old[0].shape[0], old[0].shape[1]
    rows, width = own[0].shape
    operands = (*own, *columns, *map(in_vmem, old))
    more = () if begun is None else (in_hbm(begun),)
    return pl.pallas_call(
        functools.partial(gram_kernel, other),
        out_shape=struct((height, length), F32),
        in_specs=[VMEM] * len(operands) + [ANY] * len(more),
        out_specs=ANY,
        input_output_aliases={len(operands): 0} if more else {},
        scratch_shapes=[
            pltpu.VMEM((2 * rows, height), BF16),
            pltpu.VMEM((2 * rows, width), BF16),
            pltpu.VMEM((height, width), F32),
            pltpu.SemaphoreType.DMA((height // GRAM_TILE,)),
        ],
        compiler_params=params(16),
        cost_estimate=cost(4 * rows * height * width, 8 * height * width),
        name="gram",
    )(*operands, *more)


def after(value, *others):
    return lax.optimization_barrier((value, *others))[0]


def square(stored, gram_old, w_enc, b_enc, b_dec):
    beside = flip(stored, "row", 1)
    across = flip(stored, "row", 2)
    stored, b_dec, w_out = load_first(stored, b_dec[None, :], w_enc)
    b_enc = b_enc[None, :]
    out_a, x_a = send(stored, beside, b_dec, w_out)
    shape = out_a.shape

    def pair_sum(kept, sent):
        return small(pair_kernel, "pair_sum", shape, kept, sent)

    def codes(kept, sent, far):
        return small(codes_kernel, "codes", shape, kept, sent, far, b_enc)

    def choose(here, there):
        return small(choose_kernel, "choose", shape, here, there)

    def pick(here, there):
        return small(pick_kernel, "pick", shape, here, there)

    def next_column(picked, passed):
        return small(next_kernel, "next_column", shape, picked, passed)

    sent_a = flip(out_a, "col", 1)
    kept_a, w_keep = first_keep(x_a, w_enc)
    across = after(across, kept_a)
    slant = flip(across, "row", 1)
    pair_a = pair_sum(kept_a, after(sent_a, across))
    far_a = flip(pair_a, "col", 2)
    out_b, x_b = send(across, after(slant, pair_a), b_dec, w_out)
    sent_b = flip(out_b, "col", 1)
    kept_b = keep(x_b, w_keep)
    old_top = load_half(0, kept_b, gram_old)
    far_a = after(far_a, old_top)
    pair_b = pair_sum(kept_b, after(sent_b, far_a))
    far_b = flip(pair_b, "col", 2)
    own_a = codes(kept_a, sent_a, after(far_a, pair_b))
    other_a, own_x_a = flip(own_a, "col", 1), flip(own_a, "row", 2)
    old_bottom = load_half(1, own_a, gram_old)
    own_x_a = after(own_x_a, old_bottom)
    other_x_a = flip(own_x_a, "col", 1)
    far_b = after(far_b, old_bottom, own_x_a)
    other_a = after(other_a, far_b)
    own_b = codes(kept_b, sent_b, after(far_b, other_a))
    other_b, own_x_b = flip(own_b, "col", 1), flip(own_b, "row", 2)
    held_own_a = choose(own_a, own_x_a)
    passed_own_a = flip(held_own_a, "row", 1)
    held_other_a = choose(other_a, after(other_x_a, own_b))
    passed_other_a = flip(held_other_a, "row", 1)
    pick_b = pick(own_b, after(own_x_b, held_other_a))
    passed_b = after(flip(pick_b, "row", 1), other_b)
    column_b = flip(next_column(pick_b, passed_b), "col", 1)
    rows = [own_a, other_a, own_b, other_b]
    old = [old_top, old_bottom]
    begun = gram(0, rows, [held_own_a, pick_b, passed_own_a, passed_b], old)
    columns = [held_other_a, after(column_b, begun), passed_other_a]
    return gram(1, rows, columns, old, begun)


def shards(stored, gram_old, w_enc, b_enc, b_dec):
    if lax.axis_size("row") == 4 and lax.axis_size("col") == 4:
        return square(stored, gram_old, w_enc, b_enc, b_dec)
    return plain(stored, gram_old, w_enc, b_enc, b_dec)


def solution(mesh):
    placed = (
        P(("grp", "row"), "col"),
        P(("grp", "row"), "col"),
        P("col", "row"),
        P("row"),
        P("col"),
    )
    return jax.shard_map(
        shards, mesh=mesh, in_specs=placed, out_specs=P(("grp", "row"), "col"), check_vma=False
    )
```
